32 devices in a mesh: vec: 8 (over y, x, core), field: 4 (over z).
Axes of the slice: x: 2, y: 2, z: 4, core: 2. Of those that a mesh axis runs over, the one named last changes fastest.
Arguments:
- vectors: float32 [512, 6144], P('vec', 'field'), may hold values from -6 to 6
Outputs:
- first_tensor: float32 [512, 4096], P(('vec', 'field'))
- second_tensor: float32 [512, 4096], P(('vec', 'field'))
The draws below stay inside these ranges and needn't reach their ends.
All inputs are finite; a program needn't handle non-finite values.
Results may differ from the reference program's by a relative error of at most 0.000098.
Values sent between devices are 32-bit elements; how exact they have to be, the bound alone decides.
A program may use at most 64 MiB of HBM per device.

```python
import jax
import jax.numpy as jnp
from jax import lax

NV = 64
VECS = 512
FIELDS = 6144
N_VEC = 8


def levels(own_key, extent, split, low, top_value):
    factor_of, own = 1.0, jax.random.fold_in(own_key, 6)
    for dim, blocks in split:
        steps = jnp.exp(jax.random.uniform(jax.random.fold_in(own, dim), (blocks,), jnp.float32, low / len(split), top_value / len(split)))
        factor_of = factor_of * jnp.repeat(steps, extent[dim] // blocks).reshape([-1 if axis == dim else 1 for axis in range(len(extent))])
    return factor_of


def normal_values(rng, extent, deviation, bound, pieces=(), dtype=jnp.bfloat16):
    loudness = levels(rng, extent, pieces, -0.22, 0.18) if pieces else 1.0
    values = jax.random.normal(rng, extent, jnp.float32) * deviation * loudness
    return jnp.minimum(jnp.maximum(values, -bound), bound).astype(dtype)


def setup_inputs(seed: int = 0) -> dict:
    seeds = jax.random.split(jax.random.key(seed), 2)
    vectors = normal_values(seeds[0], (VECS, FIELDS), 1.0, 6.0, ((0, 8), (1, 4)), jnp.float32)
    return {"vectors": vectors}


def triple_block(first, partner, third):
    product = (first[:, None, :] * partner[None, :, :]).reshape(first.shape[0] * partner.shape[0], first.shape[1])
    result = lax.dot_general(product, third, (((1,), (1,)), ((), ())), precision=lax.Precision.HIGHEST, preferred_element_type=jnp.float32)
    return result.reshape(first.shape[0], partner.shape[0] * third.shape[0])

def reference(vectors):
    blocks = vectors.reshape(N_VEC, NV, vectors.shape[1])
    following = jnp.roll(blocks, -1, axis=0)
    further = jnp.roll(blocks, -2, axis=0)
    previous = jnp.roll(blocks, 1, axis=0)
    scale = 1.0 / jnp.sqrt(jnp.float32(vectors.shape[1]))
    first_tensor = lax.map(lambda items: triple_block(items[0], items[1], items[2]), (blocks, following, further))
    second_tensor = lax.map(lambda items: triple_block(items[0], items[1], items[2]), (blocks, previous, following))
    first_tensor = first_tensor.reshape(N_VEC * NV, NV * NV) * scale
    second_tensor = second_tensor.reshape(N_VEC * NV, NV * NV) * scale
    return (first_tensor, second_tensor)
```

```python
import functools
import math

import jax
import jax.numpy as jnp
from jax import lax
from jax.experimental import pallas as pl
from jax.experimental.pallas import tpu as pltpu
from jax.sharding import PartitionSpec as P

MESH = pl.DeviceIdType.MESH
GATHER_PARTS = 4
TILE_COLUMNS = 256


def kernel(
    peers,
    parts,
    chunks,
    scale,
    own_ref,
    first_ref,
    second_ref,
    next_ref,
    third_ref,
    split_ref,
    partial,
    up,
    down,
    finished,
    next_send,
    next_recv,
    third_send,
    third_recv,
    up_send,
    up_recv,
    down_send,
    down_recv,
    out_send,
    out_recv,
):
    v = lax.axis_index("vec")
    z = lax.axis_index("field")
    after = lax.rem(v + 1, peers)
    before = lax.rem(v + peers - 1, peers)
    rows = own_ref.shape[0]
    owned = rows // parts
    width = first_ref.shape[1] // chunks
    per_chunk = rows // chunks
    per_group = chunks // parts
    last = parts - 1
    piece = rows // GATHER_PARTS

    barrier = pltpu.get_barrier_semaphore()
    for other in range(parts):
        for side in (before, after):
            pl.semaphore_signal(barrier, inc=1, device_id=(side, other), device_id_type=MESH)

    for near in (lax.rem(z + 1, parts), lax.rem(z + last, parts)):
        pl.semaphore_signal(barrier, inc=1, device_id=(v, near), device_id_type=MESH)
    pl.semaphore_wait(barrier, 2 * parts + 2)

    def next_copy(q):
        part = pl.ds(q * piece, piece)
        return pltpu.make_async_remote_copy(
            own_ref.at[part], next_ref.at[part], next_send.at[q], next_recv.at[q],
            device_id=(before, z), device_id_type=MESH,
        )

    def third_copy(q):
        part = pl.ds(q * piece, piece)
        return pltpu.make_async_remote_copy(
            next_ref.at[part], third_ref.at[part], third_send.at[q], third_recv.at[q],
            device_id=(before, z), device_id_type=MESH,
        )

    for q in range(GATHER_PARTS):
        next_copy(q).start()
    own = own_ref[...]
    high = own.astype(jnp.bfloat16)
    split_ref[0:rows] = high
    split_ref[rows : 2 * rows] = (own - high.astype(jnp.float32)).astype(jnp.bfloat16)
    for q in range(GATHER_PARTS):
        next_copy(q).wait_recv()
        third_copy(q).start()
    for q in range(GATHER_PARTS):
        third_copy(q).wait_recv()

    def up_copy(c, g, source):
        return pltpu.make_async_remote_copy(
            source.at[c, g], up.at[c, g], up_send.at[c, g], up_recv.at[c, g],
            device_id=(v, lax.rem(z + 1, parts)), device_id_type=MESH,
        )

    def down_copy(c, g, source):
        return pltpu.make_async_remote_copy(
            source.at[c, g], down.at[c, g], down_send.at[c, g], down_recv.at[c, g],
            device_id=(v, lax.rem(z + last, parts)), device_id_type=MESH,
        )

    def out_copy(c):
        return pltpu.make_async_remote_copy(
            finished.at[c], second_ref.at[z, lax.rem(c, per_group)], out_send.at[c],
            out_recv.at[z, lax.rem(c, per_group)],
            device_id=(after, c // per_group), device_id_type=MESH,
        )

    joined = min(TILE_COLUMNS // rows, per_chunk) if rows < TILE_COLUMNS else 1
    contract = (((1,), (1,)), ((), ()))

    def compute(c, carry):
        for t in range(per_chunk // joined):
            third = third_ref[...]
            base = c * per_chunk + t * joined
            product = jnp.concatenate(
                [next_ref[pl.ds(base + n, 1), :] * third for n in range(joined)], axis=0
            )
            top = product.astype(jnp.bfloat16)
            rest = (product - top.astype(jnp.float32)).astype(jnp.bfloat16)
            both = lax.dot_general(split_ref[...], top, contract, preferred_element_type=jnp.float32)
            small = lax.dot_general(
                split_ref[0:rows], rest, contract, preferred_element_type=jnp.float32
            )
            total = both[0:rows] + (both[rows : 2 * rows] + small)
            span = joined * rows
            for g in range(parts):
                partial[c, g, :, t * span : (t + 1) * span] = total[g * owned : (g + 1) * owned]

        @pl.when(z == 0)
        def _():
            for g in range(1, parts):
                up_copy(c, g, partial).start()

        @pl.when(z == last)
        def _():
            for g in range(last):
                down_copy(c, g, partial).start()

        return carry

    lax.fori_loop(0, chunks, compute, 0)

    def step(s, carry):
        rising = s - z + 1

        @pl.when(jnp.logical_and(z > 0, jnp.logical_and(rising >= 0, rising < chunks)))
        def _():
            def forward(g, carry):
                up_copy(rising, g, up).wait_recv()
                up[rising, g] = up[rising, g] + partial[rising, g]
                up_copy(rising, g, up).start()
                return carry

            lax.fori_loop(z + 1, parts, forward, 0)

        falling = s - (last - z) + 1

        @pl.when(jnp.logical_and(z < last, jnp.logical_and(falling >= 0, falling < chunks)))
        def _():
            def forward(g, carry):
                down_copy(falling, g, down).wait_recv()
                down[falling, g] = down[falling, g] + partial[falling, g]
                down_copy(falling, g, down).start()
                return carry

            lax.fori_loop(0, z, forward, 0)

        done = s - last + 1

        @pl.when(jnp.logical_and(done >= 0, done < chunks))
        def _():
            @pl.when(z > 0)
            def _():
                up_copy(done, z, up).wait_recv()
                partial[done, z] = partial[done, z] + up[done, z]

            @pl.when(z < last)
            def _():
                down_copy(done, z, down).wait_recv()
                partial[done, z] = partial[done, z] + down[done, z]

            result = partial[done, z] * scale
            finished[done] = result
            out_copy(done).start()
            first_ref[:, pl.ds(pl.multiple_of(done * width, width), width)] = result

        return carry

    lax.fori_loop(0, chunks + last, step, 0)

    for q in range(GATHER_PARTS):
        next_copy(q).wait_send()
        third_copy(q).wait_send()

    def drain(c, carry):
        def rise(g, carry):
            up_copy(c, g, up).wait_send()
            return carry

        def fall(g, carry):
            down_copy(c, g, down).wait_send()
            return carry

        lax.fori_loop(z + 1, parts, rise, 0)
        lax.fori_loop(0, z, fall, 0)
        out_copy(c).wait_send()
        return carry

    lax.fori_loop(0, chunks, drain, 0)

    for source in range(parts):
        for sub in range(per_group):
            pltpu.make_async_remote_copy(
                finished.at[0], second_ref.at[source, sub], out_send.at[0],
                out_recv.at[source, sub], device_id=(after, z), device_id_type=MESH,
            ).wait_recv()


def per_device(vectors):
    peers = lax.axis_size("vec")
    parts = lax.axis_size("field")
    rows, fields = vectors.shape
    owned = rows // parts
    chunks = max(8, parts)
    width = rows * rows // chunks
    scale = 1.0 / math.sqrt(fields * parts)
    per_group = chunks // parts
    vmem = pl.BlockSpec(memory_space=pltpu.VMEM)
    dma = pltpu.SemaphoreType.DMA
    first, second = pl.pallas_call(
        functools.partial(kernel, peers, parts, chunks, scale),
        out_shape=(
            jax.ShapeDtypeStruct((owned, rows * rows), jnp.float32),
            jax.ShapeDtypeStruct((parts, per_group, owned, width), jnp.float32),
        ),
        in_specs=[vmem],
        out_specs=(vmem, vmem),
        scratch_shapes=[
            pltpu.VMEM((rows, fields), jnp.float32),
            pltpu.VMEM((rows, fields), jnp.float32),
            pltpu.VMEM((2 * rows, fields), jnp.bfloat16),
            pltpu.VMEM((chunks, parts, owned, width), jnp.float32),
            pltpu.VMEM((chunks, parts, owned, width), jnp.float32),
            pltpu.VMEM((chunks, parts, owned, width), jnp.float32),
            pltpu.VMEM((chunks, owned, width), jnp.float32),
            dma((GATHER_PARTS,)),
            dma((GATHER_PARTS,)),
            dma((GATHER_PARTS,)),
            dma((GATHER_PARTS,)),
            dma((chunks, parts)),
            dma((chunks, parts)),
            dma((chunks, parts)),
            dma((chunks, parts)),
            dma((chunks,)),
            dma((parts, per_group)),
        ],
        compiler_params=pltpu.CompilerParams(
            collective_id=0, has_side_effects=True, vmem_limit_bytes=48 * 1024 * 1024
        ),
    )(vectors)
    second = second.reshape(parts, per_group, owned, width // rows, rows)
    second = second.transpose(1, 3, 0, 2, 4).reshape(owned, rows * rows)
    return (first, second)


def solution(mesh):
    return jax.shard_map(
        per_device,
        mesh=mesh,
        in_specs=(P("vec", "field"),),
        out_specs=(P(("vec", "field"), None), P(("vec", "field"), None)),
        check_vma=False,
    )
```

```python
import functools
import math

import jax
import jax.numpy as jnp
from jax import lax
from jax.experimental import pallas as pl
from jax.experimental.pallas import tpu as pltpu
from jax.sharding import PartitionSpec as P

MESH = pl.DeviceIdType.MESH
GATHER_PARTS = 4
TILE_COLUMNS = 256
LAG = 2


def kernel(
    peers,
    parts,
    chunks,
    scale,
    own_ref,
    first_ref,
    second_ref,
    next_ref,
    third_ref,
    split_ref,
    partial,
    up,
    down,
    finished,
    next_send,
    next_recv,
    third_send,
    third_recv,
    up_send,
    up_recv,
    down_send,
    down_recv,
    out_send,
    out_recv,
):
    v = lax.axis_index("vec")
    z = lax.axis_index("field")
    after = lax.rem(v + 1, peers)
    before = lax.rem(v + peers - 1, peers)
    rows = own_ref.shape[0]
    owned = rows // parts
    width = first_ref.shape[1] // chunks
    per_chunk = rows // chunks
    per_group = chunks // parts
    last = parts - 1
    piece = rows // GATHER_PARTS

    barrier = pltpu.get_barrier_semaphore()
    for other in range(parts):
        for side in (before, after):
            pl.semaphore_signal(barrier, inc=1, device_id=(side, other), device_id_type=MESH)

    for near in (lax.rem(z + 1, parts), lax.rem(z + last, parts)):
        pl.semaphore_signal(barrier, inc=1, device_id=(v, near), device_id_type=MESH)
    pl.semaphore_wait(barrier, 2 * parts + 2)

    def next_copy(q):
        part = pl.ds(q * piece, piece)
        return pltpu.make_async_remote_copy(
            own_ref.at[part], next_ref.at[part], next_send.at[q], next_recv.at[q],
            device_id=(before, z), device_id_type=MESH,
        )

    def third_copy(q):
        part = pl.ds(q * piece, piece)
        return pltpu.make_async_remote_copy(
            next_ref.at[part], third_ref.at[part], third_send.at[q], third_recv.at[q],
            device_id=(before, z), device_id_type=MESH,
        )

    for q in range(GATHER_PARTS):
        next_copy(q).start()
    own = own_ref[...]
    high = own.astype(jnp.bfloat16)
    split_ref[0:rows] = high
    split_ref[rows : 2 * rows] = (own - high.astype(jnp.float32)).astype(jnp.bfloat16)
    for q in range(GATHER_PARTS):
        next_copy(q).wait_recv()
        third_copy(q).start()
    for q in range(GATHER_PARTS):
        third_copy(q).wait_recv()

    def up_copy(c, g, source):
        return pltpu.make_async_remote_copy(
            source.at[c, g], up.at[c, g], up_send.at[c, g], up_recv.at[c, g],
            device_id=(v, lax.rem(z + 1, parts)), device_id_type=MESH,
        )

    def down_copy(c, g, source):
        return pltpu.make_async_remote_copy(
            source.at[c, g], down.at[c, g], down_send.at[c, g], down_recv.at[c, g],
            device_id=(v, lax.rem(z + last, parts)), device_id_type=MESH,
        )

    def out_copy(c):
        return pltpu.make_async_remote_copy(
            finished.at[c], second_ref.at[z, lax.rem(c, per_group)], out_send.at[c],
            out_recv.at[z, lax.rem(c, per_group)],
            device_id=(after, c // per_group), device_id_type=MESH,
        )

    joined = min(TILE_COLUMNS // rows, per_chunk) if rows < TILE_COLUMNS else 1
    contract = (((1,), (1,)), ((), ()))

    def compute(c, carry):
        for t in range(per_chunk // joined):
            third = third_ref[...]
            base = c * per_chunk + t * joined
            product = jnp.concatenate(
                [next_ref[pl.ds(base + n, 1), :] * third for n in range(joined)], axis=0
            )
            top = product.astype(jnp.bfloat16)
            rest = (product - top.astype(jnp.float32)).astype(jnp.bfloat16)
            both = lax.dot_general(split_ref[...], top, contract, preferred_element_type=jnp.float32)
            small = lax.dot_general(
                split_ref[0:rows], rest, contract, preferred_element_type=jnp.float32
            )
            total = both[0:rows] + (both[rows : 2 * rows] + small)
            span = joined * rows
            for g in range(parts):
                partial[c, g, :, t * span : (t + 1) * span] = total[g * owned : (g + 1) * owned]

        @pl.when(z == 0)
        def _():
            for g in range(last, 0, -1):
                up_copy(c, g, partial).start()

        @pl.when(z == last)
        def _():
            for g in range(last):
                down_copy(c, g, partial).start()

        return carry

    def step(s, carry):
        rising = s - z + 1

        @pl.when(jnp.logical_and(z > 0, jnp.logical_and(rising >= 0, rising < chunks)))
        def _():
            def forward(n, carry):
                g = last - n
                up_copy(rising, g, up).wait_recv()
                up[rising, g] = up[rising, g] + partial[rising, g]
                up_copy(rising, g, up).start()
                return carry

            lax.fori_loop(0, last - z, forward, 0)

        falling = s - (last - z) + 1

        @pl.when(jnp.logical_and(z < last, jnp.logical_and(falling >= 0, falling < chunks)))
        def _():
            def forward(g, carry):
                down_copy(falling, g, down).wait_recv()
                down[falling, g] = down[falling, g] + partial[falling, g]
                down_copy(falling, g, down).start()
                return carry

            lax.fori_loop(0, z, forward, 0)

        done = s - last + 1

        @pl.when(jnp.logical_and(done >= 0, done < chunks))
        def _():
            @pl.when(z > 0)
            def _():
                up_copy(done, z, up).wait_recv()
                partial[done, z] = partial[done, z] + up[done, z]

            @pl.when(z < last)
            def _():
                down_copy(done, z, down).wait_recv()
                partial[done, z] = partial[done, z] + down[done, z]

            result = partial[done, z] * scale
            finished[done] = result
            out_copy(done).start()
            first_ref[:, pl.ds(pl.multiple_of(done * width, width), width)] = result

        return carry

    def both_at(s, carry):
        @pl.when(s < chunks)
        def _():
            compute(s, 0)

        return step(s - LAG, carry)

    lax.fori_loop(0, chunks + last + LAG, both_at, 0)

    for q in range(GATHER_PARTS):
        next_copy(q).wait_send()
        third_copy(q).wait_send()

    def drain(c, carry):
        def rise(g, carry):
            up_copy(c, g, up).wait_send()
            return carry

        def fall(g, carry):
            down_copy(c, g, down).wait_send()
            return carry

        lax.fori_loop(z + 1, parts, rise, 0)
        lax.fori_loop(0, z, fall, 0)
        out_copy(c).wait_send()
        return carry

    lax.fori_loop(0, chunks, drain, 0)

    for source in range(parts):
        for sub in range(per_group):
            pltpu.make_async_remote_copy(
                finished.at[0], second_ref.at[source, sub], out_send.at[0],
                out_recv.at[source, sub], device_id=(after, z), device_id_type=MESH,
            ).wait_recv()


def per_device(vectors):
    peers = lax.axis_size("vec")
    parts = lax.axis_size("field")
    rows, fields = vectors.shape
    owned = rows // parts
    chunks = max(8, parts)
    width = rows * rows // chunks
    scale = 1.0 / math.sqrt(fields * parts)
    per_group = chunks // parts
    vmem = pl.BlockSpec(memory_space=pltpu.VMEM)
    dma = pltpu.SemaphoreType.DMA
    first, second = pl.pallas_call(
        functools.partial(kernel, peers, parts, chunks, scale),
        out_shape=(
            jax.ShapeDtypeStruct((owned, rows * rows), jnp.float32),
            jax.ShapeDtypeStruct((parts, per_group, owned, width), jnp.float32),
        ),
        in_specs=[vmem],
        out_specs=(vmem, vmem),
        scratch_shapes=[
            pltpu.VMEM((rows, fields), jnp.float32),
            pltpu.VMEM((rows, fields), jnp.float32),
            pltpu.VMEM((2 * rows, fields), jnp.bfloat16),
            pltpu.VMEM((chunks, parts, owned, width), jnp.float32),
            pltpu.VMEM((chunks, parts, owned, width), jnp.float32),
            pltpu.VMEM((chunks, parts, owned, width), jnp.float32),
            pltpu.VMEM((chunks, owned, width), jnp.float32),
            dma((GATHER_PARTS,)),
            dma((GATHER_PARTS,)),
            dma((GATHER_PARTS,)),
            dma((GATHER_PARTS,)),
            dma((chunks, parts)),
            dma((chunks, parts)),
            dma((chunks, parts)),
            dma((chunks, parts)),
            dma((chunks,)),
            dma((parts, per_group)),
        ],
        compiler_params=pltpu.CompilerParams(
            collective_id=0, has_side_effects=True, vmem_limit_bytes=48 * 1024 * 1024
        ),
    )(vectors)
    second = second.reshape(parts, per_group, owned, width // rows, rows)
    second = second.transpose(1, 3, 0, 2, 4).reshape(owned, rows * rows)
    return (first, second)


def solution(mesh):
    return jax.shard_map(
        per_device,
        mesh=mesh,
        in_specs=(P("vec", "field"),),
        out_specs=(P(("vec", "field"), None), P(("vec", "field"), None)),
        check_vma=False,
    )
```

```python
import functools
import math

import jax
import jax.numpy as jnp
from jax import lax
from jax.experimental import pallas as pl
from jax.experimental.pallas import tpu as pltpu
from jax.sharding import PartitionSpec as P

MESH = pl.DeviceIdType.MESH
GATHER_PARTS = 4
TILE_COLUMNS = 256
LAG = 3


def kernel(
    peers,
    parts,
    chunks,
    scale,
    own_ref,
    first_ref,
    second_ref,
    next_ref,
    third_ref,
    split_ref,
    partial,
    up,
    down,
    finished,
    next_send,
    next_recv,
    third_send,
    third_recv,
    up_send,
    up_recv,
    down_send,
    down_recv,
    out_send,
    out_recv,
):
    v = lax.axis_index("vec")
    z = lax.axis_index("field")
    after = lax.rem(v + 1, peers)
    before = lax.rem(v + peers - 1, peers)
    rows = own_ref.shape[0]
    owned = rows // parts
    width = first_ref.shape[1] // chunks
    per_chunk = rows // chunks
    per_group = chunks // parts
    last = parts - 1
    piece = rows // GATHER_PARTS

    barrier = pltpu.get_barrier_semaphore()
    for other in range(parts):
        for side in (before, after):
            pl.semaphore_signal(barrier, inc=1, device_id=(side, other), device_id_type=MESH)

    for near in (lax.rem(z + 1, parts), lax.rem(z + last, parts)):
        pl.semaphore_signal(barrier, inc=1, device_id=(v, near), device_id_type=MESH)
    pl.semaphore_wait(barrier, 2 * parts + 2)

    def place(c):
        return lax.rem(c, parts) * per_group + c // parts

    def next_copy(q):
        part = pl.ds(q * piece, piece)
        return pltpu.make_async_remote_copy(
            own_ref.at[part], next_ref.at[part], next_send.at[q], next_recv.at[q],
            device_id=(before, z), device_id_type=MESH,
        )

    def third_copy(q):
        part = pl.ds(q * piece, piece)
        return pltpu.make_async_remote_copy(
            next_ref.at[part], third_ref.at[part], third_send.at[q], third_recv.at[q],
            device_id=(before, z), device_id_type=MESH,
        )

    for q in range(GATHER_PARTS):
        next_copy(q).start()
    own = own_ref[...]
    high = own.astype(jnp.bfloat16)
    split_ref[0:rows] = high
    split_ref[rows : 2 * rows] = (own - high.astype(jnp.float32)).astype(jnp.bfloat16)
    for q in range(GATHER_PARTS):
        next_copy(q).wait_recv()
        third_copy(q).start()
    for q in range(GATHER_PARTS):
        third_copy(q).wait_recv()

    def up_copy(c, g, source):
        return pltpu.make_async_remote_copy(
            source.at[c, g], up.at[c, g], up_send.at[c, g], up_recv.at[c, g],
            device_id=(v, lax.rem(z + 1, parts)), device_id_type=MESH,
        )

    def down_copy(c, g, source):
        return pltpu.make_async_remote_copy(
            source.at[c, g], down.at[c, g], down_send.at[c, g], down_recv.at[c, g],
            device_id=(v, lax.rem(z + last, parts)), device_id_type=MESH,
        )

    def out_copy(c):
        return pltpu.make_async_remote_copy(
            finished.at[c], second_ref.at[z, c // parts], out_send.at[c],
            out_recv.at[z, c // parts],
            device_id=(after, lax.rem(c, parts)), device_id_type=MESH,
        )

    joined = min(TILE_COLUMNS // rows, per_chunk) if rows < TILE_COLUMNS else 1
    contract = (((1,), (1,)), ((), ()))

    def compute(c, carry):
        for t in range(per_chunk // joined):
            third = third_ref[...]
            base = place(c) * per_chunk + t * joined
            product = jnp.concatenate(
                [next_ref[pl.ds(base + n, 1), :] * third for n in range(joined)], axis=0
            )
            top = product.astype(jnp.bfloat16)
            rest = (product - top.astype(jnp.float32)).astype(jnp.bfloat16)
            both = lax.dot_general(split_ref[...], top, contract, preferred_element_type=jnp.float32)
            small = lax.dot_general(
                split_ref[0:rows], rest, contract, preferred_element_type=jnp.float32
            )
            total = both[0:rows] + (both[rows : 2 * rows] + small)
            span = joined * rows
            for g in range(parts):
                partial[c, g, :, t * span : (t + 1) * span] = total[g * owned : (g + 1) * owned]

        @pl.when(z == 0)
        def _():
            for g in range(last, 0, -1):
                up_copy(c, g, partial).start()

        @pl.when(z == last)
        def _():
            for g in range(last):
                down_copy(c, g, partial).start()

        return carry

    def step(s, carry):
        rising = s - z + 1

        @pl.when(jnp.logical_and(z > 0, jnp.logical_and(rising >= 0, rising < chunks)))
        def _():
            def forward(n, carry):
                g = last - n
                up_copy(rising, g, up).wait_recv()
                up[rising, g] = up[rising, g] + partial[rising, g]
                up_copy(rising, g, up).start()
                return carry

            lax.fori_loop(0, last - z, forward, 0)

        falling = s - (last - z) + 1

        @pl.when(jnp.logical_and(z < last, jnp.logical_and(falling >= 0, falling < chunks)))
        def _():
            def forward(g, carry):
                down_copy(falling, g, down).wait_recv()
                down[falling, g] = down[falling, g] + partial[falling, g]
                down_copy(falling, g, down).start()
                return carry

            lax.fori_loop(0, z, forward, 0)

        done = s - last + 1

        @pl.when(jnp.logical_and(done >= 0, done < chunks))
        def _():
            @pl.when(z > 0)
            def _():
                up_copy(done, z, up).wait_recv()
                partial[done, z] = partial[done, z] + up[done, z]

            @pl.when(z < last)
            def _():
                down_copy(done, z, down).wait_recv()
                partial[done, z] = partial[done, z] + down[done, z]

            result = partial[done, z] * scale
            finished[done] = result
            out_copy(done).start()
            first_ref[:, pl.ds(pl.multiple_of(place(done) * width, width), width)] = result

        return carry

    def both_at(s, carry):
        @pl.when(s < chunks)
        def _():
            compute(s, 0)

        return step(s - LAG, carry)

    lax.fori_loop(0, chunks + last + LAG, both_at, 0)

    for q in range(GATHER_PARTS):
        next_copy(q).wait_send()
        third_copy(q).wait_send()

    def drain(c, carry):
        def rise(g, carry):
            up_copy(c, g, up).wait_send()
            return carry

        def fall(g, carry):
            down_copy(c, g, down).wait_send()
            return carry

        lax.fori_loop(z + 1, parts, rise, 0)
        lax.fori_loop(0, z, fall, 0)
        out_copy(c).wait_send()
        return carry

    lax.fori_loop(0, chunks, drain, 0)

    for source in range(parts):
        for sub in range(per_group):
            pltpu.make_async_remote_copy(
                finished.at[0], second_ref.at[source, sub], out_send.at[0],
                out_recv.at[source, sub], device_id=(after, z), device_id_type=MESH,
            ).wait_recv()


def per_device(vectors):
    peers = lax.axis_size("vec")
    parts = lax.axis_size("field")
    rows, fields = vectors.shape
    owned = rows // parts
    chunks = max(16, parts)
    width = rows * rows // chunks
    scale = 1.0 / math.sqrt(fields * parts)
    per_group = chunks // parts
    vmem = pl.BlockSpec(memory_space=pltpu.VMEM)
    dma = pltpu.SemaphoreType.DMA
    first, second = pl.pallas_call(
        functools.partial(kernel, peers, parts, chunks, scale),
        out_shape=(
            jax.ShapeDtypeStruct((owned, rows * rows), jnp.float32),
            jax.ShapeDtypeStruct((parts, per_group, owned, width), jnp.float32),
        ),
        in_specs=[vmem],
        out_specs=(vmem, vmem),
        scratch_shapes=[
            pltpu.VMEM((rows, fields), jnp.float32),
            pltpu.VMEM((rows, fields), jnp.float32),
            pltpu.VMEM((2 * rows, fields), jnp.bfloat16),
            pltpu.VMEM((chunks, parts, owned, width), jnp.float32),
            pltpu.VMEM((chunks, parts, owned, width), jnp.float32),
            pltpu.VMEM((chunks, parts, owned, width), jnp.float32),
            pltpu.VMEM((chunks, owned, width), jnp.float32),
            dma((GATHER_PARTS,)),
            dma((GATHER_PARTS,)),
            dma((GATHER_PARTS,)),
            dma((GATHER_PARTS,)),
            dma((chunks, parts)),
            dma((chunks, parts)),
            dma((chunks, parts)),
            dma((chunks, parts)),
            dma((chunks,)),
            dma((parts, per_group)),
        ],
        compiler_params=pltpu.CompilerParams(
            collective_id=0, has_side_effects=True, vmem_limit_bytes=48 * 1024 * 1024
        ),
    )(vectors)
    second = second.reshape(parts, per_group, owned, width // rows, rows)
    second = second.transpose(1, 3, 0, 2, 4).reshape(owned, rows * rows)
    return (first, second)


def solution(mesh):
    return jax.shard_map(
        per_device,
        mesh=mesh,
        in_specs=(P("vec", "field"),),
        out_specs=(P(("vec", "field"), None), P(("vec", "field"), None)),
        check_vma=False,
    )
```

```python
import functools
import math

import jax
import jax.numpy as jnp
from jax import lax
from jax.experimental import pallas as pl
from jax.experimental.pallas import tpu as pltpu
from jax.sharding import PartitionSpec as P

MESH = pl.DeviceIdType.MESH
GATHER_PARTS = 4
TILE_COLUMNS = 256
LAG = 2


def kernel(
    peers,
    parts,
    chunks,
    scale,
    own_ref,
    first_ref,
    second_ref,
    next_ref,
    third_ref,
    split_ref,
    partial,
    up,
    down,
    finished,
    next_send,
    next_recv,
    third_send,
    third_recv,
    up_send,
    up_recv,
    down_send,
    down_recv,
    out_send,
    out_recv,
):
    v = lax.axis_index("vec")
    z = lax.axis_index("field")
    after = lax.rem(v + 1, peers)
    before = lax.rem(v + peers - 1, peers)
    rows = own_ref.shape[0]
    owned = rows // parts
    width = first_ref.shape[1] // chunks
    per_chunk = rows // chunks
    per_group = chunks // parts
    last = parts - 1
    piece = rows // GATHER_PARTS

    barrier = pltpu.get_barrier_semaphore()
    for other in range(parts):
        for side in (before, after):
            pl.semaphore_signal(barrier, inc=1, device_id=(side, other), device_id_type=MESH)

    for near in (lax.rem(z + 1, parts), lax.rem(z + last, parts)):
        pl.semaphore_signal(barrier, inc=1, device_id=(v, near), device_id_type=MESH)
    pl.semaphore_wait(barrier, 2 * parts + 2)

    def next_copy(q):
        part = pl.ds(q * piece, piece)
        return pltpu.make_async_remote_copy(
            own_ref.at[part], next_ref.at[part], next_send.at[q], next_recv.at[q],
            device_id=(before, z), device_id_type=MESH,
        )

    def third_copy(q):
        part = pl.ds(q * piece, piece)
        return pltpu.make_async_remote_copy(
            next_ref.at[part], third_ref.at[part], third_send.at[q], third_recv.at[q],
            device_id=(before, z), device_id_type=MESH,
        )

    for q in range(GATHER_PARTS):
        next_copy(q).start()
    own = own_ref[...]
    high = own.astype(jnp.bfloat16)
    split_ref[0:rows] = high
    split_ref[rows : 2 * rows] = (own - high.astype(jnp.float32)).astype(jnp.bfloat16)
    for q in range(GATHER_PARTS):
        next_copy(q).wait_recv()
        third_copy(q).start()
    for q in range(GATHER_PARTS):
        third_copy(q).wait_recv()

    def up_copy(c, d, source):
        return pltpu.make_async_remote_copy(
            source.at[c, d + 1 : parts], up.at[c, d + 1 : parts], up_send.at[c], up_recv.at[c],
            device_id=(v, lax.rem(z + 1, parts)), device_id_type=MESH,
        )

    def down_copy(c, d, source):
        return pltpu.make_async_remote_copy(
            source.at[c, 0:d], down.at[c, 0:d], down_send.at[c], down_recv.at[c],
            device_id=(v, lax.rem(z + last, parts)), device_id_type=MESH,
        )

    def out_copy(c):
        return pltpu.make_async_remote_copy(
            finished.at[c], second_ref.at[z, lax.rem(c, per_group)], out_send.at[c],
            out_recv.at[z, lax.rem(c, per_group)],
            device_id=(after, c // per_group), device_id_type=MESH,
        )

    joined = min(TILE_COLUMNS // rows, per_chunk) if rows < TILE_COLUMNS else 1
    contract = (((1,), (1,)), ((), ()))

    def compute(c, carry):
        for t in range(per_chunk // joined):
            third = third_ref[...]
            base = c * per_chunk + t * joined
            product = jnp.concatenate(
                [next_ref[pl.ds(base + n, 1), :] * third for n in range(joined)], axis=0
            )
            top = product.astype(jnp.bfloat16)
            rest = (product - top.astype(jnp.float32)).astype(jnp.bfloat16)
            both = lax.dot_general(split_ref[...], top, contract, preferred_element_type=jnp.float32)
            small = lax.dot_general(
                split_ref[0:rows], rest, contract, preferred_element_type=jnp.float32
            )
            total = both[0:rows] + (both[rows : 2 * rows] + small)
            span = joined * rows
            for g in range(parts):
                partial[c, g, :, t * span : (t + 1) * span] = total[g * owned : (g + 1) * owned]

        @pl.when(z == 0)
        def _():
            up_copy(c, 0, partial).start()

        @pl.when(z == last)
        def _():
            down_copy(c, last, partial).start()

        return carry

    def step(s, carry):
        rising = s - z + 1
        falling = s - (last - z) + 1

        for d in range(1, parts):
            @pl.when(jnp.logical_and(z == d, jnp.logical_and(rising >= 0, rising < chunks)))
            def _(d=d):
                up_copy(rising, d - 1, up).wait_recv()
                if d < last:
                    up[rising, d + 1 : parts] = (
                        up[rising, d + 1 : parts] + partial[rising, d + 1 : parts]
                    )
                    up_copy(rising, d, up).start()

        for d in range(last):
            @pl.when(jnp.logical_and(z == d, jnp.logical_and(falling >= 0, falling < chunks)))
            def _(d=d):
                down_copy(falling, d + 1, down).wait_recv()
                if d > 0:
                    down[falling, 0:d] = down[falling, 0:d] + partial[falling, 0:d]
                    down_copy(falling, d, down).start()

        done = s - last + 1

        @pl.when(jnp.logical_and(done >= 0, done < chunks))
        def _():
            @pl.when(z > 0)
            def _():
                partial[done, z] = partial[done, z] + up[done, z]

            @pl.when(z < last)
            def _():
                partial[done, z] = partial[done, z] + down[done, z]

            result = partial[done, z] * scale
            finished[done] = result
            out_copy(done).start()
            first_ref[:, pl.ds(pl.multiple_of(done * width, width), width)] = result

        return carry

    def both_at(s, carry):
        @pl.when(s < chunks)
        def _():
            compute(s, 0)

        return step(s - LAG, carry)

    lax.fori_loop(0, chunks + last + LAG, both_at, 0)

    for q in range(GATHER_PARTS):
        next_copy(q).wait_send()
        third_copy(q).wait_send()

    def drain(c, carry):
        for d in range(parts):
            @pl.when(z == d)
            def _(d=d):
                if d < last:
                    up_copy(c, d, up).wait_send()
                if d > 0:
                    down_copy(c, d, down).wait_send()

        out_copy(c).wait_send()
        return carry

    lax.fori_loop(0, chunks, drain, 0)

    for source in range(parts):
        for sub in range(per_group):
            pltpu.make_async_remote_copy(
                finished.at[0], second_ref.at[source, sub], out_send.at[0],
                out_recv.at[source, sub], device_id=(after, z), device_id_type=MESH,
            ).wait_recv()


def per_device(vectors):
    peers = lax.axis_size("vec")
    parts = lax.axis_size("field")
    rows, fields = vectors.shape
    owned = rows // parts
    chunks = max(8, parts)
    width = rows * rows // chunks
    scale = 1.0 / math.sqrt(fields * parts)
    per_group = chunks // parts
    vmem = pl.BlockSpec(memory_space=pltpu.VMEM)
    dma = pltpu.SemaphoreType.DMA
    first, second = pl.pallas_call(
        functools.partial(kernel, peers, parts, chunks, scale),
        out_shape=(
            jax.ShapeDtypeStruct((owned, rows * rows), jnp.float32),
            jax.ShapeDtypeStruct((parts, per_group, owned, width), jnp.float32),
        ),
        in_specs=[vmem],
        out_specs=(vmem, vmem),
        scratch_shapes=[
            pltpu.VMEM((rows, fields), jnp.float32),
            pltpu.VMEM((rows, fields), jnp.float32),
            pltpu.VMEM((2 * rows, fields), jnp.bfloat16),
            pltpu.VMEM((chunks, parts, owned, width), jnp.float32),
            pltpu.VMEM((chunks, parts, owned, width), jnp.float32),
            pltpu.VMEM((chunks, parts, owned, width), jnp.float32),
            pltpu.VMEM((chunks, owned, width), jnp.float32),
            dma((GATHER_PARTS,)),
            dma((GATHER_PARTS,)),
            dma((GATHER_PARTS,)),
            dma((GATHER_PARTS,)),
            dma((chunks,)),
            dma((chunks,)),
            dma((chunks,)),
            dma((chunks,)),
            dma((chunks,)),
            dma((parts, per_group)),
        ],
        compiler_params=pltpu.CompilerParams(
            collective_id=0, has_side_effects=True, vmem_limit_bytes=48 * 1024 * 1024
        ),
    )(vectors)
    second = second.reshape(parts, per_group, owned, width // rows, rows)
    second = second.transpose(1, 3, 0, 2, 4).reshape(owned, rows * rows)
    return (first, second)


def solution(mesh):
    return jax.shard_map(
        per_device,
        mesh=mesh,
        in_specs=(P("vec", "field"),),
        out_specs=(P(("vec", "field"), None), P(("vec", "field"), None)),
        check_vma=False,
    )
```

```python
import functools
import math

import jax
import jax.numpy as jnp
from jax import lax
from jax.experimental import pallas as pl
from jax.experimental.pallas import tpu as pltpu
from jax.sharding import PartitionSpec as P

MESH = pl.DeviceIdType.MESH
GATHER_PARTS = 8
TILE_COLUMNS = 256
LAG = 3


def kernel(
    peers,
    parts,
    chunks,
    scale,
    own_ref,
    first_ref,
    second_ref,
    next_ref,
    third_ref,
    split_ref,
    partial,
    up,
    down,
    finished,
    next_send,
    next_recv,
    third_send,
    third_recv,
    up_send,
    up_recv,
    down_send,
    down_recv,
    out_send,
    out_recv,
):
    v = lax.axis_index("vec")
    z = lax.axis_index("field")
    after = lax.rem(v + 1, peers)
    before = lax.rem(v + peers - 1, peers)
    rows = own_ref.shape[0]
    owned = rows // parts
    width = first_ref.shape[1] // chunks
    per_chunk = rows // chunks
    per_group = chunks // parts
    last = parts - 1
    piece = rows // GATHER_PARTS

    barrier = pltpu.get_barrier_semaphore()
    for other in range(parts):
        for side in (before, after):
            pl.semaphore_signal(barrier, inc=1, device_id=(side, other), device_id_type=MESH)

    for near in (lax.rem(z + 1, parts), lax.rem(z + last, parts)):
        pl.semaphore_signal(barrier, inc=1, device_id=(v, near), device_id_type=MESH)
    pl.semaphore_wait(barrier, 2 * parts + 2)

    def next_copy(q):
        part = pl.ds(q * piece, piece)
        return pltpu.make_async_remote_copy(
            own_ref.at[part], next_ref.at[part], next_send.at[q], next_recv.at[q],
            device_id=(before, z), device_id_type=MESH,
        )

    def third_copy(q):
        part = pl.ds(q * piece, piece)
        return pltpu.make_async_remote_copy(
            next_ref.at[part], third_ref.at[part], third_send.at[q], third_recv.at[q],
            device_id=(before, z), device_id_type=MESH,
        )

    for q in range(GATHER_PARTS):
        next_copy(q).start()
    own = own_ref[...]
    high = own.astype(jnp.bfloat16)
    split_ref[0:rows] = high
    split_ref[rows : 2 * rows] = (own - high.astype(jnp.float32)).astype(jnp.bfloat16)
    for q in range(GATHER_PARTS):
        next_copy(q).wait_recv()
        third_copy(q).start()
    for q in range(GATHER_PARTS):
        third_copy(q).wait_recv()

    def up_copy(c, g, source):
        return pltpu.make_async_remote_copy(
            source.at[c, g], up.at[c, g], up_send.at[c, g], up_recv.at[c, g],
            device_id=(v, lax.rem(z + 1, parts)), device_id_type=MESH,
        )

    def down_copy(c, g, source):
        return pltpu.make_async_remote_copy(
            source.at[c, g], down.at[c, g], down_send.at[c, g], down_recv.at[c, g],
            device_id=(v, lax.rem(z + last, parts)), device_id_type=MESH,
        )

    def out_copy(c):
        return pltpu.make_async_remote_copy(
            finished.at[c], second_ref.at[z, lax.rem(c, per_group)], out_send.at[c],
            out_recv.at[z, lax.rem(c, per_group)],
            device_id=(after, c // per_group), device_id_type=MESH,
        )

    joined = min(TILE_COLUMNS // rows, per_chunk) if rows < TILE_COLUMNS else 1
    contract = (((1,), (1,)), ((), ()))

    def compute(c, carry):
        for t in range(per_chunk // joined):
            third = third_ref[...]
            base = c * per_chunk + t * joined
            product = jnp.concatenate(
                [next_ref[pl.ds(base + n, 1), :] * third for n in range(joined)], axis=0
            )
            top = product.astype(jnp.bfloat16)
            rest = (product - top.astype(jnp.float32)).astype(jnp.bfloat16)
            both = lax.dot_general(split_ref[...], top, contract, preferred_element_type=jnp.float32)
            small = lax.dot_general(
                split_ref[0:rows], rest, contract, preferred_element_type=jnp.float32
            )
            total = both[0:rows] + (both[rows : 2 * rows] + small)
            span = joined * rows
            for g in range(parts):
                partial[c, g, :, t * span : (t + 1) * span] = total[g * owned : (g + 1) * owned]

        @pl.when(z == 0)
        def _():
            for g in range(last, 0, -1):
                up_copy(c, g, partial).start()

        @pl.when(z == last)
        def _():
            for g in range(last):
                down_copy(c, g, partial).start()

        return carry

    def step(s, carry):
        rising = s - z + 1

        @pl.when(jnp.logical_and(z > 0, jnp.logical_and(rising >= 0, rising < chunks)))
        def _():
            def forward(n, carry):
                g = last - n
                up_copy(rising, g, up).wait_recv()
                up[rising, g] = up[rising, g] + partial[rising, g]
                up_copy(rising, g, up).start()
                return carry

            lax.fori_loop(0, last - z, forward, 0)

        falling = s - (last - z) + 1

        @pl.when(jnp.logical_and(z < last, jnp.logical_and(falling >= 0, falling < chunks)))
        def _():
            def forward(g, carry):
                down_copy(falling, g, down).wait_recv()
                down[falling, g] = down[falling, g] + partial[falling, g]
                down_copy(falling, g, down).start()
                return carry

            lax.fori_loop(0, z, forward, 0)

        done = s - last + 1

        @pl.when(jnp.logical_and(done >= 0, done < chunks))
        def _():
            @pl.when(z > 0)
            def _():
                up_copy(done, z, up).wait_recv()
                partial[done, z] = partial[done, z] + up[done, z]

            @pl.when(z < last)
            def _():
                down_copy(done, z, down).wait_recv()
                partial[done, z] = partial[done, z] + down[done, z]

            result = partial[done, z] * scale
            finished[done] = result
            out_copy(done).start()
            first_ref[:, pl.ds(pl.multiple_of(done * width, width), width)] = result

        return carry

    def both_at(s, carry):
        @pl.when(s < chunks)
        def _():
            compute(s, 0)

        return step(s - LAG, carry)

    lax.fori_loop(0, chunks + last + LAG, both_at, 0)

    for q in range(GATHER_PARTS):
        next_copy(q).wait_send()
        third_copy(q).wait_send()

    def drain(c, carry):
        def rise(g, carry):
            up_copy(c, g, up).wait_send()
            return carry

        def fall(g, carry):
            down_copy(c, g, down).wait_send()
            return carry

        lax.fori_loop(z + 1, parts, rise, 0)
        lax.fori_loop(0, z, fall, 0)
        out_copy(c).wait_send()
        return carry

    lax.fori_loop(0, chunks, drain, 0)

    for source in range(parts):
        for sub in range(per_group):
            pltpu.make_async_remote_copy(
                finished.at[0], second_ref.at[source, sub], out_send.at[0],
                out_recv.at[source, sub], device_id=(after, z), device_id_type=MESH,
            ).wait_recv()


def per_device(vectors):
    peers = lax.axis_size("vec")
    parts = lax.axis_size("field")
    rows, fields = vectors.shape
    owned = rows // parts
    chunks = max(8, parts)
    width = rows * rows // chunks
    scale = 1.0 / math.sqrt(fields * parts)
    per_group = chunks // parts
    vmem = pl.BlockSpec(memory_space=pltpu.VMEM)
    dma = pltpu.SemaphoreType.DMA
    first, second = pl.pallas_call(
        functools.partial(kernel, peers, parts, chunks, scale),
        out_shape=(
            jax.ShapeDtypeStruct((owned, rows * rows), jnp.float32),
            jax.ShapeDtypeStruct((parts, per_group, owned, width), jnp.float32),
        ),
        in_specs=[vmem],
        out_specs=(vmem, vmem),
        scratch_shapes=[
            pltpu.VMEM((rows, fields), jnp.float32),
            pltpu.VMEM((rows, fields), jnp.float32),
            pltpu.VMEM((2 * rows, fields), jnp.bfloat16),
            pltpu.VMEM((chunks, parts, owned, width), jnp.float32),
            pltpu.VMEM((chunks, parts, owned, width), jnp.float32),
            pltpu.VMEM((chunks, parts, owned, width), jnp.float32),
            pltpu.VMEM((chunks, owned, width), jnp.float32),
            dma((GATHER_PARTS,)),
            dma((GATHER_PARTS,)),
            dma((GATHER_PARTS,)),
            dma((GATHER_PARTS,)),
            dma((chunks, parts)),
            dma((chunks, parts)),
            dma((chunks, parts)),
            dma((chunks, parts)),
            dma((chunks,)),
            dma((parts, per_group)),
        ],
        compiler_params=pltpu.CompilerParams(
            collective_id=0, has_side_effects=True, vmem_limit_bytes=48 * 1024 * 1024
        ),
    )(vectors)
    second = second.reshape(parts, per_group, owned, width // rows, rows)
    second = second.transpose(1, 3, 0, 2, 4).reshape(owned, rows * rows)
    return (first, second)


def solution(mesh):
    return jax.shard_map(
        per_device,
        mesh=mesh,
        in_specs=(P("vec", "field"),),
        out_specs=(P(("vec", "field"), None), P(("vec", "field"), None)),
        check_vma=False,
    )
```

```python
import functools
import math

import jax
import jax.numpy as jnp
from jax import lax
from jax.experimental import pallas as pl
from jax.experimental.pallas import tpu as pltpu
from jax.sharding import PartitionSpec as P

MESH = pl.DeviceIdType.MESH
GATHER_PARTS = 4
TILE_COLUMNS = 256
LAG = 2


def kernel(
    peers,
    parts,
    chunks,
    scale,
    own_ref,
    first_ref,
    second_ref,
    next_ref,
    third_ref,
    local_ref,
    split_ref,
    partial,
    up,
    down,
    finished,
    next_send,
    next_recv,
    third_send,
    third_recv,
    up_send,
    up_recv,
    down_send,
    down_recv,
    out_send,
    out_recv,
    local_done,
):
    v = lax.axis_index("vec")
    z = lax.axis_index("field")
    after = lax.rem(v + 1, peers)
    before = lax.rem(v + peers - 1, peers)
    rows = own_ref.shape[0]
    owned = rows // parts
    width = first_ref.shape[1] // chunks
    per_chunk = rows // chunks
    per_group = chunks // parts
    last = parts - 1
    piece = rows // GATHER_PARTS

    local = pltpu.make_async_copy(own_ref, local_ref, local_done)
    local.start()
    barrier = pltpu.get_barrier_semaphore()
    for other in range(parts):
        for side in (before, after):
            pl.semaphore_signal(barrier, inc=1, device_id=(side, other), device_id_type=MESH)

    for near in (lax.rem(z + 1, parts), lax.rem(z + last, parts)):
        pl.semaphore_signal(barrier, inc=1, device_id=(v, near), device_id_type=MESH)
    pl.semaphore_wait(barrier, 2 * parts + 2)

    def next_copy(q):
        part = pl.ds(q * piece, piece)
        return pltpu.make_async_remote_copy(
            own_ref.at[part], next_ref.at[part], next_send.at[q], next_recv.at[q],
            device_id=(before, z), device_id_type=MESH,
        )

    def third_copy(q):
        part = pl.ds(q * piece, piece)
        return pltpu.make_async_remote_copy(
            next_ref.at[part], third_ref.at[part], third_send.at[q], third_recv.at[q],
            device_id=(before, z), device_id_type=MESH,
        )

    for q in range(GATHER_PARTS):
        next_copy(q).start()
    local.wait()
    own = local_ref[...]
    high = own.astype(jnp.bfloat16)
    split_ref[0:rows] = high
    split_ref[rows : 2 * rows] = (own - high.astype(jnp.float32)).astype(jnp.bfloat16)
    for q in range(GATHER_PARTS):
        next_copy(q).wait_recv()
        third_copy(q).start()
    for q in range(GATHER_PARTS):
        third_copy(q).wait_recv()

    def up_copy(c, g, source):
        return pltpu.make_async_remote_copy(
            source.at[c, g], up.at[c, g], up_send.at[c, g], up_recv.at[c, g],
            device_id=(v, lax.rem(z + 1, parts)), device_id_type=MESH,
        )

    def down_copy(c, g, source):
        return pltpu.make_async_remote_copy(
            source.at[c, g], down.at[c, g], down_send.at[c, g], down_recv.at[c, g],
            device_id=(v, lax.rem(z + last, parts)), device_id_type=MESH,
        )

    def out_copy(c):
        return pltpu.make_async_remote_copy(
            finished.at[c], second_ref.at[z, lax.rem(c, per_group)], out_send.at[c],
            out_recv.at[z, lax.rem(c, per_group)],
            device_id=(after, c // per_group), device_id_type=MESH,
        )

    joined = min(TILE_COLUMNS // rows, per_chunk) if rows < TILE_COLUMNS else 1
    contract = (((1,), (1,)), ((), ()))

    def compute(c, carry):
        for t in range(per_chunk // joined):
            third = third_ref[...]
            base = c * per_chunk + t * joined
            product = jnp.concatenate(
                [next_ref[pl.ds(base + n, 1), :] * third for n in range(joined)], axis=0
            )
            top = product.astype(jnp.bfloat16)
            rest = (product - top.astype(jnp.float32)).astype(jnp.bfloat16)
            both = lax.dot_general(split_ref[...], top, contract, preferred_element_type=jnp.float32)
            small = lax.dot_general(
                split_ref[0:rows], rest, contract, preferred_element_type=jnp.float32
            )
            total = both[0:rows] + (both[rows : 2 * rows] + small)
            span = joined * rows
            for g in range(parts):
                partial[c, g, :, t * span : (t + 1) * span] = total[g * owned : (g + 1) * owned]

        @pl.when(z == 0)
        def _():
            for g in range(last, 0, -1):
                up_copy(c, g, partial).start()

        @pl.when(z == last)
        def _():
            for g in range(last):
                down_copy(c, g, partial).start()

        return carry

    def step(s, carry):
        rising = s - z + 1

        @pl.when(jnp.logical_and(z > 0, jnp.logical_and(rising >= 0, rising < chunks)))
        def _():
            def forward(n, carry):
                g = last - n
                up_copy(rising, g, up).wait_recv()
                up[rising, g] = up[rising, g] + partial[rising, g]
                up_copy(rising, g, up).start()
                return carry

            lax.fori_loop(0, last - z, forward, 0)

        falling = s - (last - z) + 1

        @pl.when(jnp.logical_and(z < last, jnp.logical_and(falling >= 0, falling < chunks)))
        def _():
            def forward(g, carry):
                down_copy(falling, g, down).wait_recv()
                down[falling, g] = down[falling, g] + partial[falling, g]
                down_copy(falling, g, down).start()
                return carry

            lax.fori_loop(0, z, forward, 0)

        done = s - last + 1

        @pl.when(jnp.logical_and(done >= 0, done < chunks))
        def _():
            @pl.when(z > 0)
            def _():
                up_copy(done, z, up).wait_recv()
                partial[done, z] = partial[done, z] + up[done, z]

            @pl.when(z < last)
            def _():
                down_copy(done, z, down).wait_recv()
                partial[done, z] = partial[done, z] + down[done, z]

            result = partial[done, z] * scale
            finished[done] = result
            out_copy(done).start()
            first_ref[:, pl.ds(pl.multiple_of(done * width, width), width)] = result

        return carry

    def both_at(s, carry):
        @pl.when(s < chunks)
        def _():
            compute(s, 0)

        return step(s - LAG, carry)

    lax.fori_loop(0, chunks + last + LAG, both_at, 0)

    for q in range(GATHER_PARTS):
        next_copy(q).wait_send()
        third_copy(q).wait_send()

    def drain(c, carry):
        def rise(g, carry):
            up_copy(c, g, up).wait_send()
            return carry

        def fall(g, carry):
            down_copy(c, g, down).wait_send()
            return carry

        lax.fori_loop(z + 1, parts, rise, 0)
        lax.fori_loop(0, z, fall, 0)
        out_copy(c).wait_send()
        return carry

    lax.fori_loop(0, chunks, drain, 0)

    for source in range(parts):
        for sub in range(per_group):
            pltpu.make_async_remote_copy(
                finished.at[0], second_ref.at[source, sub], out_send.at[0],
                out_recv.at[source, sub], device_id=(after, z), device_id_type=MESH,
            ).wait_recv()


def per_device(vectors):
    peers = lax.axis_size("vec")
    parts = lax.axis_size("field")
    rows, fields = vectors.shape
    owned = rows // parts
    chunks = max(8, parts)
    width = rows * rows // chunks
    scale = 1.0 / math.sqrt(fields * parts)
    per_group = chunks // parts
    vmem = pl.BlockSpec(memory_space=pltpu.VMEM)
    dma = pltpu.SemaphoreType.DMA
    first, second = pl.pallas_call(
        functools.partial(kernel, peers, parts, chunks, scale),
        out_shape=(
            jax.ShapeDtypeStruct((owned, rows * rows), jnp.float32),
            jax.ShapeDtypeStruct((parts, per_group, owned, width), jnp.float32),
        ),
        in_specs=[pl.BlockSpec(memory_space=pl.ANY)],
        out_specs=(vmem, vmem),
        scratch_shapes=[
            pltpu.VMEM((rows, fields), jnp.float32),
            pltpu.VMEM((rows, fields), jnp.float32),
            pltpu.VMEM((rows, fields), jnp.float32),
            pltpu.VMEM((2 * rows, fields), jnp.bfloat16),
            pltpu.VMEM((chunks, parts, owned, width), jnp.float32),
            pltpu.VMEM((chunks, parts, owned, width), jnp.float32),
            pltpu.VMEM((chunks, parts, owned, width), jnp.float32),
            pltpu.VMEM((chunks, owned, width), jnp.float32),
            dma((GATHER_PARTS,)),
            dma((GATHER_PARTS,)),
            dma((GATHER_PARTS,)),
            dma((GATHER_PARTS,)),
            dma((chunks, parts)),
            dma((chunks, parts)),
            dma((chunks, parts)),
            dma((chunks, parts)),
            dma((chunks,)),
            dma((parts, per_group)),
            dma,
        ],
        compiler_params=pltpu.CompilerParams(
            collective_id=0, has_side_effects=True, vmem_limit_bytes=48 * 1024 * 1024
        ),
    )(vectors)
    second = second.reshape(parts, per_group, owned, width // rows, rows)
    second = second.transpose(1, 3, 0, 2, 4).reshape(owned, rows * rows)
    return (first, second)


def solution(mesh):
    return jax.shard_map(
        per_device,
        mesh=mesh,
        in_specs=(P("vec", "field"),),
        out_specs=(P(("vec", "field"), None), P(("vec", "field"), None)),
        check_vma=False,
    )
```

```python
import functools
import math

import jax
import jax.numpy as jnp
from jax import lax
from jax.experimental import pallas as pl
from jax.experimental.pallas import tpu as pltpu
from jax.sharding import PartitionSpec as P

MESH = pl.DeviceIdType.MESH
GATHER_PARTS = 2
TILE_COLUMNS = 256
LAG = 2


def kernel(
    peers,
    parts,
    chunks,
    scale,
    own_ref,
    first_ref,
    second_ref,
    next_ref,
    third_ref,
    local_ref,
    split_ref,
    partial,
    up,
    down,
    finished,
    next_send,
    next_recv,
    third_send,
    third_recv,
    up_send,
    up_recv,
    down_send,
    down_recv,
    out_send,
    out_recv,
    local_done,
):
    v = lax.axis_index("vec")
    z = lax.axis_index("field")
    after = lax.rem(v + 1, peers)
    before = lax.rem(v + peers - 1, peers)
    rows = own_ref.shape[0]
    owned = rows // parts
    width = first_ref.shape[1] // chunks
    per_chunk = rows // chunks
    per_group = chunks // parts
    last = parts - 1
    piece = rows // GATHER_PARTS

    local = pltpu.make_async_copy(own_ref, local_ref, local_done)
    local.start()
    barrier = pltpu.get_barrier_semaphore()
    for other in range(parts):
        for side in (before, after):
            pl.semaphore_signal(barrier, inc=1, device_id=(side, other), device_id_type=MESH)

    for near in (lax.rem(z + 1, parts), lax.rem(z + last, parts)):
        pl.semaphore_signal(barrier, inc=1, device_id=(v, near), device_id_type=MESH)
    pl.semaphore_wait(barrier, 2 * parts + 2)

    def next_copy(q):
        part = pl.ds(q * piece, piece)
        return pltpu.make_async_remote_copy(
            own_ref.at[part], next_ref.at[part], next_send.at[q], next_recv.at[q],
            device_id=(before, z), device_id_type=MESH,
        )

    def third_copy(q):
        part = pl.ds(q * piece, piece)
        return pltpu.make_async_remote_copy(
            next_ref.at[part], third_ref.at[part], third_send.at[q], third_recv.at[q],
            device_id=(before, z), device_id_type=MESH,
        )

    for q in range(GATHER_PARTS):
        next_copy(q).start()
    local.wait()
    own = local_ref[...]
    high = own.astype(jnp.bfloat16)
    split_ref[0:rows] = high
    split_ref[rows : 2 * rows] = (own - high.astype(jnp.float32)).astype(jnp.bfloat16)
    for q in range(GATHER_PARTS):
        next_copy(q).wait_recv()
        third_copy(q).start()
    for q in range(GATHER_PARTS):
        third_copy(q).wait_recv()

    def up_copy(c, g, source):
        return pltpu.make_async_remote_copy(
            source.at[c, g], up.at[c, g], up_send.at[c, g], up_recv.at[c, g],
            device_id=(v, lax.rem(z + 1, parts)), device_id_type=MESH,
        )

    def down_copy(c, g, source):
        return pltpu.make_async_remote_copy(
            source.at[c, g], down.at[c, g], down_send.at[c, g], down_recv.at[c, g],
            device_id=(v, lax.rem(z + last, parts)), device_id_type=MESH,
        )

    def out_copy(c):
        return pltpu.make_async_remote_copy(
            finished.at[c], second_ref.at[z, lax.rem(c, per_group)], out_send.at[c],
            out_recv.at[z, lax.rem(c, per_group)],
            device_id=(after, c // per_group), device_id_type=MESH,
        )

    joined = min(TILE_COLUMNS // rows, per_chunk) if rows < TILE_COLUMNS else 1
    contract = (((1,), (1,)), ((), ()))

    def compute(c, carry):
        for t in range(per_chunk // joined):
            third = third_ref[...]
            base = c * per_chunk + t * joined
            product = jnp.concatenate(
                [next_ref[pl.ds(base + n, 1), :] * third for n in range(joined)], axis=0
            )
            top = product.astype(jnp.bfloat16)
            rest = (product - top.astype(jnp.float32)).astype(jnp.bfloat16)
            both = lax.dot_general(split_ref[...], top, contract, preferred_element_type=jnp.float32)
            small = lax.dot_general(
                split_ref[0:rows], rest, contract, preferred_element_type=jnp.float32
            )
            total = both[0:rows] + (both[rows : 2 * rows] + small)
            span = joined * rows
            for g in range(parts):
                partial[c, g, :, t * span : (t + 1) * span] = total[g * owned : (g + 1) * owned]

        @pl.when(z == 0)
        def _():
            for g in range(last, 0, -1):
                up_copy(c, g, partial).start()

        @pl.when(z == last)
        def _():
            for g in range(last):
                down_copy(c, g, partial).start()

        return carry

    def step(s, carry):
        rising = s - z + 1

        @pl.when(jnp.logical_and(z > 0, jnp.logical_and(rising >= 0, rising < chunks)))
        def _():
            def forward(n, carry):
                g = last - n
                up_copy(rising, g, up).wait_recv()
                up[rising, g] = up[rising, g] + partial[rising, g]
                up_copy(rising, g, up).start()
                return carry

            lax.fori_loop(0, last - z, forward, 0)

        falling = s - (last - z) + 1

        @pl.when(jnp.logical_and(z < last, jnp.logical_and(falling >= 0, falling < chunks)))
        def _():
            def forward(g, carry):
                down_copy(falling, g, down).wait_recv()
                down[falling, g] = down[falling, g] + partial[falling, g]
                down_copy(falling, g, down).start()
                return carry

            lax.fori_loop(0, z, forward, 0)

        done = s - last + 1

        @pl.when(jnp.logical_and(done >= 0, done < chunks))
        def _():
            @pl.when(z > 0)
            def _():
                up_copy(done, z, up).wait_recv()
                partial[done, z] = partial[done, z] + up[done, z]

            @pl.when(z < last)
            def _():
                down_copy(done, z, down).wait_recv()
                partial[done, z] = partial[done, z] + down[done, z]

            result = partial[done, z] * scale
            finished[done] = result
            out_copy(done).start()
            first_ref[:, pl.ds(pl.multiple_of(done * width, width), width)] = result

        return carry

    def both_at(s, carry):
        @pl.when(s < chunks)
        def _():
            compute(s, 0)

        return step(s - LAG, carry)

    lax.fori_loop(0, chunks + last + LAG, both_at, 0)

    for q in range(GATHER_PARTS):
        next_copy(q).wait_send()
        third_copy(q).wait_send()

    def drain(c, carry):
        def rise(g, carry):
            up_copy(c, g, up).wait_send()
            return carry

        def fall(g, carry):
            down_copy(c, g, down).wait_send()
            return carry

        lax.fori_loop(z + 1, parts, rise, 0)
        lax.fori_loop(0, z, fall, 0)
        out_copy(c).wait_send()
        return carry

    lax.fori_loop(0, chunks, drain, 0)

    for source in range(parts):
        for sub in range(per_group):
            pltpu.make_async_remote_copy(
                finished.at[0], second_ref.at[source, sub], out_send.at[0],
                out_recv.at[source, sub], device_id=(after, z), device_id_type=MESH,
            ).wait_recv()


def per_device(vectors):
    peers = lax.axis_size("vec")
    parts = lax.axis_size("field")
    rows, fields = vectors.shape
    owned = rows // parts
    chunks = max(8, parts)
    width = rows * rows // chunks
    scale = 1.0 / math.sqrt(fields * parts)
    per_group = chunks // parts
    vmem = pl.BlockSpec(memory_space=pltpu.VMEM)
    dma = pltpu.SemaphoreType.DMA
    first, second = pl.pallas_call(
        functools.partial(kernel, peers, parts, chunks, scale),
        out_shape=(
            jax.ShapeDtypeStruct((owned, rows * rows), jnp.float32),
            jax.ShapeDtypeStruct((parts, per_group, owned, width), jnp.float32),
        ),
        in_specs=[pl.BlockSpec(memory_space=pl.ANY)],
        out_specs=(vmem, vmem),
        scratch_shapes=[
            pltpu.VMEM((rows, fields), jnp.float32),
            pltpu.VMEM((rows, fields), jnp.float32),
            pltpu.VMEM((rows, fields), jnp.float32),
            pltpu.VMEM((2 * rows, fields), jnp.bfloat16),
            pltpu.VMEM((chunks, parts, owned, width), jnp.float32),
            pltpu.VMEM((chunks, parts, owned, width), jnp.float32),
            pltpu.VMEM((chunks, parts, owned, width), jnp.float32),
            pltpu.VMEM((chunks, owned, width), jnp.float32),
            dma((GATHER_PARTS,)),
            dma((GATHER_PARTS,)),
            dma((GATHER_PARTS,)),
            dma((GATHER_PARTS,)),
            dma((chunks, parts)),
            dma((chunks, parts)),
            dma((chunks, parts)),
            dma((chunks, parts)),
            dma((chunks,)),
            dma((parts, per_group)),
            dma,
        ],
        compiler_params=pltpu.CompilerParams(
            collective_id=0, has_side_effects=True, vmem_limit_bytes=48 * 1024 * 1024
        ),
    )(vectors)
    second = second.reshape(parts, per_group, owned, width // rows, rows)
    second = second.transpose(1, 3, 0, 2, 4).reshape(owned, rows * rows)
    return (first, second)


def solution(mesh):
    return jax.shard_map(
        per_device,
        mesh=mesh,
        in_specs=(P("vec", "field"),),
        out_specs=(P(("vec", "field"), None), P(("vec", "field"), None)),
        check_vma=False,
    )
```
